256 devices in a mesh: row: 8 (over x, y_lo), col: 16 (over z, core), dp: 2 (over y_hi).
Axes of the slice: x: 4, y: 4 (y_hi: 2, y_lo: 2; y = y_hi * 2 + y_lo), z: 8, core: 2. Of those that a mesh axis runs over, the one named last changes fastest.
Arguments:
- layer_input: bfloat16 [2048, 12288], P(('dp', 'col'), 'row'), parts along dimension 0, may hold values from -6 to 6
- layer_norm_gain: float32 [12288], P('row'), may hold values from 0.1 to 1.9
- w_qkv: bfloat16 [12288, 18432], P('row', 'col'), may hold values from -16 to 16
- w_out: bfloat16 [6144, 12288], P('col', 'row'), may hold values from -0.078125 to 0.078125
- out_grad: bfloat16 [2048, 12288], P(('dp', 'col'), 'row'), parts along dimension 0, may hold values from -6 to 6
Outputs:
- input_gradient: bfloat16 [2048, 12288], P(('dp', 'col'), 'row'), parts along dimension 0
- gain_gradient: float32 [24576], P(('dp', 'row')), parts along dimension 0
- grad_wqkv: bfloat16 [24576, 18432], P(('dp', 'row'), 'col'), parts along dimension 0
- grad_wout: bfloat16 [12288, 12288], P(('dp', 'col'), 'row'), parts along dimension 0
The draws below stay inside these ranges and needn't reach their ends.
There are 2 independent parts, one for each index of `dp`. The reference program is written for one: setup_inputs(seed, part) draws one part's arguments, and reference() takes and returns one part's arrays. A program takes and returns all parts, laid end to end along the dimension named above; an argument that names none is the same for every part. Nothing has to cross between parts.
All inputs are finite; a program needn't handle non-finite values.
Results may differ from the reference program's by a relative error of at most 0.0098.
Values may be sent and summed in bfloat16 or wider, within the bound.
No kernel may reach another device: no remote copies, remote signals or barrier semaphores. Data moves between devices by JAX's collectives and lax.ppermute only.
A program may use at most 128 MiB of HBM per device.

```python
import math
import jax
import jax.numpy as jnp
from jax import lax

D = 12288
HEADS = 48
HS = 128
TOKENS = 1024


def draw_w_qkv(key, part):
    key = jax.random.fold_in(key, 11)
    base_key = jax.random.fold_in(key, 0)
    base = jax.random.truncated_normal(base_key, -6.0, 6.0, (D, HEADS, 3, HS), jnp.float32) * D ** (-0.5)
    return base.reshape(D, HEADS * 3 * HS).astype(jnp.bfloat16)


def steps_of(key, extent, pieces, least, high):
    def one(axis_at, blocks):
        steps = jax.random.uniform(jax.random.fold_in(jax.random.fold_in(key, 6), axis_at), (blocks,), jnp.float32, least / len(pieces), high / len(pieces))
        return jnp.repeat(jnp.exp(steps), extent[axis_at] // blocks).reshape((-1,) + (1,) * (len(extent) - axis_at - 1))

    level = one(*pieces[0])
    for cut in pieces[1:]:
        level = level * one(*cut)
    return level


def normal_values(stream_key, extent, width, most, cuts=(), kind=jnp.bfloat16):
    values = jax.random.normal(stream_key, extent, jnp.float32) * width
    if len(cuts) > 0:
        values = steps_of(stream_key, extent, cuts, -0.22, 0.18) * values
    return jnp.clip(values, min=-most, max=most).astype(kind)


def setup_inputs(seed: int = 0, part: int = 0) -> dict:
    key_of = jax.random.split(jax.random.key(seed), 6)
    part_splits = jax.random.split(jax.random.fold_in(key_of[5], part), 6)
    layer_input = normal_values(part_splits[0], (TOKENS, D), 1.0, 6.0, ((0, 16), (1, 8)))
    layer_norm_gain = jnp.clip(1.0 + 0.18 * jax.random.normal(key_of[1], (D,), jnp.float32), 0.1, 1.9)
    w_qkv = draw_w_qkv(jax.random.fold_in(key_of[5], 71), part)
    w_out = normal_values(key_of[3], (HEADS * HS, D), (HEADS * HS) ** -0.5, 0.078125, ((0, 16), (1, 8)))
    out_grad = normal_values(part_splits[4], (TOKENS, D), 1.0, 6.0, ((0, 16), (1, 8)))
    return dict(layer_input=layer_input, layer_norm_gain=layer_norm_gain, w_qkv=w_qkv, w_out=w_out, out_grad=out_grad)


EPS = 1e-05

def reference(layer_input, layer_norm_gain, w_qkv, w_out, out_grad):
    scale = 1.0 / math.sqrt(HS)
    input_float = layer_input.astype(jnp.float32)
    average = lax.optimization_barrier(jnp.mean(input_float, axis=1, keepdims=True))
    centered_input = input_float - average
    variance = lax.optimization_barrier(jnp.mean(centered_input * centered_input, axis=1, keepdims=True))
    inverse_deviation = lax.rsqrt(variance + EPS)
    standardized_input = centered_input * inverse_deviation
    normalized_output = (standardized_input * layer_norm_gain[None, :]).astype(jnp.bfloat16)
    qkv = jnp.dot(normalized_output, w_qkv, preferred_element_type=jnp.float32).astype(jnp.bfloat16)
    qkv = qkv.reshape(TOKENS, HEADS, 3, HS)
    heads_first = jnp.transpose(qkv, (1, 2, 0, 3))
    position = jnp.arange(TOKENS)
    allowed = position[None, :] <= position[:, None]

    def probs_of(query, keys):
        scores = jnp.dot(query, keys.T, preferred_element_type=jnp.float32) * scale
        scores = jnp.where(allowed, scores, -jnp.inf)
        highest = lax.optimization_barrier(jnp.max(scores, axis=1, keepdims=True))
        powers = jnp.exp(scores - highest)
        return powers / lax.optimization_barrier(jnp.sum(powers, axis=1, keepdims=True))

    def forward_head(block):
        probs = probs_of(block[0], block[1])
        return jnp.dot(probs.astype(jnp.bfloat16), block[2], preferred_element_type=jnp.float32).astype(jnp.bfloat16)
    context_heads = lax.map(forward_head, heads_first)
    context = jnp.transpose(context_heads, (1, 0, 2)).reshape(TOKENS, HEADS * HS)
    grad_wout = jnp.dot(context.T, out_grad, preferred_element_type=jnp.float32).astype(jnp.bfloat16)
    d_context = jnp.dot(out_grad, w_out.T, preferred_element_type=jnp.float32).astype(jnp.bfloat16)
    d_context_heads = jnp.transpose(d_context.reshape(TOKENS, HEADS, HS), (1, 0, 2))

    def backward_head(items):
        block, grad = items
        query, keys, values = (block[0], block[1], block[2])
        probs = probs_of(query, keys)
        probs_b = probs.astype(jnp.bfloat16)
        d_probs = jnp.dot(grad, values.T, preferred_element_type=jnp.float32)
        delta = lax.optimization_barrier(jnp.sum(probs * d_probs, axis=1, keepdims=True))
        d_scores = (probs * (d_probs - delta) * scale).astype(jnp.bfloat16)
        d_query = jnp.dot(d_scores, keys, preferred_element_type=jnp.float32).astype(jnp.bfloat16)
        d_keys = jnp.dot(d_scores.T, query, preferred_element_type=jnp.float32).astype(jnp.bfloat16)
        d_values = jnp.dot(probs_b.T, grad, preferred_element_type=jnp.float32).astype(jnp.bfloat16)
        return jnp.stack([d_query, d_keys, d_values], axis=0)
    d_heads = lax.map(backward_head, (heads_first, d_context_heads))
    d_qkv = jnp.transpose(d_heads, (2, 0, 1, 3)).reshape(TOKENS, 3 * HEADS * HS)
    grad_wqkv = jnp.dot(normalized_output.T, d_qkv, preferred_element_type=jnp.float32).astype(jnp.bfloat16)
    normalized_gradient = jnp.dot(d_qkv, w_qkv.T, preferred_element_type=jnp.float32)
    gain_gradient = lax.optimization_barrier(jnp.sum(normalized_gradient * standardized_input, axis=0))
    scaled_gradient = normalized_gradient * layer_norm_gain[None, :]
    first_term = lax.optimization_barrier(jnp.mean(scaled_gradient, axis=1, keepdims=True))
    second_term = lax.optimization_barrier(jnp.mean(scaled_gradient * standardized_input, axis=1, keepdims=True))
    input_gradient = (inverse_deviation * (scaled_gradient - first_term - standardized_input * second_term)).astype(jnp.bfloat16)
    return (input_gradient, gain_gradient, grad_wqkv, grad_wout)
```

```python
import functools
import math

import jax
import jax.numpy as jnp
from jax import lax
from jax.experimental import pallas as pl
from jax.experimental.pallas import tpu as pltpu
from jax.sharding import PartitionSpec as P

HS = 128
EPS = 1e-05
F32 = jnp.float32
BF16 = jnp.bfloat16
QB = 256
VMEM_LIMIT = 48 * 1024 * 1024


def row_perm(dx, dy):
    return [(r, ((r // 2 + dx) % 4) * 2 + ((r % 2) ^ dy)) for r in range(8)]


def col_perm(dz, dc):
    return [(c, ((c // 2 + dz) % 8) * 2 + ((c % 2) ^ dc)) for c in range(16)]


def to_row(v, dx, dy):
    return lax.ppermute(v, "row", row_perm(dx, dy))


def to_col(v, dz, dc):
    return lax.ppermute(v, "col", col_perm(dz, dc))


def gather_col(own):
    half = own.shape[0] // 2
    up, down = [own], [own]
    for _ in range(3):
        up.append(to_col(up[-1], 1, 0))
        down.append(to_col(down[-1], -1, 0))
    far = jnp.concatenate([to_col(up[3][:half], 1, 0), to_col(down[3][half:], -1, 0)], axis=0)
    mine = jnp.concatenate([own, down[1], down[2], down[3], far, up[3], up[2], up[1]], axis=0)
    return jnp.concatenate([mine, to_col(mine, 0, 1)], axis=0)


def scatter_col(partial):
    tokens = partial.shape[0]
    block = tokens // 16
    half = block // 2
    other = to_col(partial[tokens // 2 :], 0, 1)
    mine = partial[: tokens // 2].astype(F32) + other.astype(F32)
    blocks = [mine[p * block : (p + 1) * block] for p in range(8)]
    up = to_col(blocks[4][:half].astype(BF16), 1, 0)
    down = to_col(blocks[4][half:].astype(BF16), -1, 0)
    up_sum = jnp.concatenate([blocks[3][:half] + up.astype(F32), blocks[3][half:]], axis=0)
    down_sum = jnp.concatenate([blocks[5][:half], blocks[5][half:] + down.astype(F32)], axis=0)
    up = to_col(up_sum.astype(BF16), 1, 0)
    down = to_col(down_sum.astype(BF16), -1, 0)
    up = to_col((blocks[2] + up.astype(F32)).astype(BF16), 1, 0)
    down = to_col((blocks[6] + down.astype(F32)).astype(BF16), -1, 0)
    up = to_col((blocks[1] + up.astype(F32)).astype(BF16), 1, 0)
    down = to_col((blocks[7] + down.astype(F32)).astype(BF16), -1, 0)
    return blocks[0] + up.astype(F32) + down.astype(F32)


def exchange(v, axis):
    n = lax.axis_size(axis)
    return lax.all_to_all(jnp.broadcast_to(v[None], (n, *v.shape)), axis, 0, 0)


def sum_row(partial):
    tokens = partial.shape[0]
    sent = lax.all_to_all(partial.astype(BF16), "row", 0, 0, tiled=True)
    own = jnp.sum(sent.reshape(8, tokens // 8, -1).astype(F32), axis=0).astype(BF16)
    across = to_row(own, 0, 1)
    pair = jnp.concatenate([own, across], axis=0)
    return own, across, to_row(pair, -1, 0), to_row(pair, 1, 0), to_row(pair, 2, 0)


def block_starts(block):
    r = lax.axis_index("row")
    c = lax.axis_index("col")
    x, y, z, core = r // 2, r % 2, c // 2, c % 2

    def place(b):
        other = b // 8
        return (((z + b) % 8) * 2 + (core + other) % 2) * block

    b = jnp.arange(16, dtype=jnp.int32)
    owners = []
    for dx, dy in ((0, 0), (0, 1), (1, 0), (1, 1), (3, 0), (3, 1), (2, 0), (2, 1)):
        owners.append(((x + dx) % 4) * 2 + (y + dy) % 2)
    owner = jnp.stack(owners).astype(jnp.int32)
    piece = (2 * owner[:, None] + jnp.arange(2, dtype=jnp.int32)[None]).reshape(16)
    return jnp.concatenate([place(piece), place(b)]).astype(jnp.int32)


def attention_kernel(
    block, starts, q0, q1, q2, q3, q4, g0, g1, g2, g3, g4, u_ref, ctx_ref, dqkv_ref, term_ref, qkv, dout, dkv, dall, ctx_s
):
    head = pl.program_id(0)
    tokens = qkv.shape[0]
    scale = 1.0 / math.sqrt(HS)
    nt = (((1,), (1,)), ((), ()))

    at = 0
    for pq, pg in ((q0, g0), (q1, g1), (q2, g2), (q3, g3), (q4, g4)):
        for i in range(pq.shape[0] // block):
            to = pl.ds(pl.multiple_of(starts[at], block), block)
            qkv[to, :] = pq[i * block : (i + 1) * block, :]
            dout[to, :] = pg[i * block : (i + 1) * block, :]
            at += 1

    dkv[...] = jnp.zeros_like(dkv)
    k_t = qkv[:, HS : 2 * HS].T
    v_t = qkv[:, 2 * HS : 3 * HS].T
    key_at = lax.broadcasted_iota(jnp.int32, (QB, QB), 0)
    query_at = lax.broadcasted_iota(jnp.int32, (QB, QB), 1)
    for i in range(tokens // QB):
        lo, hi = i * QB, (i + 1) * QB
        query = qkv[lo:hi, :HS]
        grad = dout[lo:hi, :]
        keys = qkv[:hi, HS : 2 * HS]
        values = qkv[:hi, 2 * HS : 3 * HS]
        s = lax.dot_general(keys, query, nt, preferred_element_type=F32) * (scale * math.log2(math.e))
        last = jnp.where(key_at <= query_at, s[lo:hi], -jnp.inf)
        s = jnp.concatenate([s[:lo], last], axis=0) if i else last
        powers = jnp.exp2(s - jnp.max(s, axis=0, keepdims=True))
        probs = powers * (1.0 / jnp.sum(powers, axis=0, keepdims=True))
        probs_b = probs.astype(BF16)
        d_probs = lax.dot_general(values, grad, nt, preferred_element_type=F32)
        delta = jnp.sum(probs * d_probs, axis=0, keepdims=True)
        d_scores = (probs * (d_probs - delta) * scale).astype(BF16)
        ctx_s[lo:hi, :] = jnp.dot(v_t[:, :hi], probs_b, preferred_element_type=F32).T.astype(BF16)
        dall[lo:hi, :HS] = jnp.dot(k_t[:, :hi], d_scores, preferred_element_type=F32).T.astype(BF16)
        dkv[:hi, :HS] += jnp.dot(d_scores, query, preferred_element_type=F32)
        dkv[:hi, HS:] += jnp.dot(probs_b, grad, preferred_element_type=F32)
    dall[:, HS:] = dkv[...].astype(BF16)

    for b in range(16):
        src = pl.ds(pl.multiple_of(starts[16 + b], block), block)
        to = slice(b * block, (b + 1) * block)
        piece = dall[src, :]
        dqkv_ref[to, :] = piece
        ctx_ref[to, :] = ctx_s[src, :]
        wide = piece.astype(F32)
        first = jnp.sum(wide * u_ref[...], axis=1, keepdims=True)
        second = jnp.sum(wide * qkv[src, :].astype(F32), axis=1, keepdims=True)
        lane = lax.broadcasted_iota(jnp.int32, (block, HS), 1)
        both = jnp.where(lane == 0, first, jnp.where(lane == 1, second, 0.0))

        @pl.when(head == 0)
        def _():
            term_ref[to, :] = both

        @pl.when(head > 0)
        def _():
            term_ref[to, :] += both


def attention(starts, qkv_pieces, grad_pieces, u):
    tokens = sum(p.shape[0] for p in qkv_pieces)
    width = qkv_pieces[0].shape[1]
    heads = width // (3 * HS)
    block = tokens // 16

    def by_head(rows, cols):
        return pl.BlockSpec((rows, cols), lambda h, s: (0, h))

    return pl.pallas_call(
        functools.partial(attention_kernel, block),
        grid_spec=pltpu.PrefetchScalarGridSpec(
            num_scalar_prefetch=1,
            grid=(heads,),
            in_specs=[by_head(p.shape[0], 3 * HS) for p in qkv_pieces]
            + [by_head(p.shape[0], HS) for p in grad_pieces]
            + [by_head(1, 3 * HS)],
            out_specs=[
                by_head(tokens, HS),
                by_head(tokens, 3 * HS),
                pl.BlockSpec((tokens, HS), lambda h, s: (0, 0)),
            ],
            scratch_shapes=[
                pltpu.VMEM((tokens, 3 * HS), BF16),
                pltpu.VMEM((tokens, HS), BF16),
                pltpu.VMEM((tokens, 2 * HS), F32),
                pltpu.VMEM((tokens, 3 * HS), BF16),
                pltpu.VMEM((tokens, HS), BF16),
            ],
        ),
        out_shape=[
            jax.ShapeDtypeStruct((tokens, heads * HS), BF16),
            jax.ShapeDtypeStruct((tokens, width), BF16),
            jax.ShapeDtypeStruct((tokens, HS), F32),
        ],
        compiler_params=pltpu.CompilerParams(vmem_limit_bytes=VMEM_LIMIT),
        cost_estimate=pl.CostEstimate(
            flops=heads * tokens * tokens * HS * 12 * 5 // 8,
            bytes_accessed=tokens * width * 6,
            transcendentals=heads * tokens * tokens * 5 // 8,
        ),
        name="attention",
    )(starts, *qkv_pieces, *grad_pieces, u)


def input_kernel(features, dqkv_ref, w_ref, normed_ref, gain_ref, term_ref, out_ref, gain_grad_ref):
    nt = (((1,), (1,)), ((), ()))
    d_normed = lax.dot_general(dqkv_ref[...], w_ref[...], nt, preferred_element_type=F32)
    gain = gain_ref[...]
    inverse = 1.0 / gain
    normed = normed_ref[...].astype(F32)
    first = term_ref[:, 0:1] * (1.0 / features)
    second = term_ref[:, 1:2] * (1.0 / features)
    out_ref[...] = (d_normed * gain - first - normed * inverse * second).astype(BF16)
    part = jnp.sum(d_normed * normed, axis=0, keepdims=True) * inverse

    @pl.when(pl.program_id(0) == 0)
    def _():
        gain_grad_ref[...] = part

    @pl.when(pl.program_id(0) > 0)
    def _():
        gain_grad_ref[...] += part


def input_partial(features, d_qkv, w_qkv, normed, gain, terms):
    tokens, width = d_qkv.shape
    here = w_qkv.shape[0]
    rows = 256
    return pl.pallas_call(
        functools.partial(input_kernel, features),
        grid=(tokens // rows,),
        in_specs=[
            pl.BlockSpec((rows, width), lambda i: (i, 0)),
            pl.BlockSpec((here, width), lambda i: (0, 0)),
            pl.BlockSpec((rows, here), lambda i: (i, 0)),
            pl.BlockSpec((1, here), lambda i: (0, 0)),
            pl.BlockSpec((rows, HS), lambda i: (i, 0)),
        ],
        out_specs=[
            pl.BlockSpec((rows, here), lambda i: (i, 0)),
            pl.BlockSpec((1, here), lambda i: (0, 0)),
        ],
        out_shape=[
            jax.ShapeDtypeStruct((tokens, here), BF16),
            jax.ShapeDtypeStruct((1, here), F32),
        ],
        compiler_params=pltpu.CompilerParams(vmem_limit_bytes=VMEM_LIMIT),
        cost_estimate=pl.CostEstimate(
            flops=2 * tokens * width * here,
            bytes_accessed=2 * (tokens * width + width * here + 2 * tokens * here),
            transcendentals=0,
        ),
        name="input_partial",
    )(d_qkv, w_qkv, normed, gain, terms)


def shards(layer_input, gain, w_qkv, w_out, out_grad):
    block, here = layer_input.shape
    features = here * lax.axis_size("row")
    grad_all = gather_col(out_grad)

    x = layer_input.astype(F32)
    mean_here = jnp.sum(x, axis=1) / here
    apart = x - mean_here[:, None]
    squares_here = jnp.sum(apart * apart, axis=1)
    u_here = jnp.sum(w_qkv.astype(F32) * gain[:, None], axis=0)
    told = exchange(jnp.concatenate([mean_here, squares_here, u_here]), "row")
    means, squares = told[:, :block], told[:, block : 2 * block]
    mean = jnp.mean(means, axis=0)
    variance = (jnp.sum(squares, axis=0) + here * jnp.sum((means - mean) ** 2, axis=0)) / features
    rstd = lax.rsqrt(variance + EPS)
    u = jnp.sum(told[:, 2 * block :], axis=0)[None]
    normed = ((x - mean[:, None]) * rstd[:, None] * gain[None]).astype(BF16)
    normed_all = gather_col(normed)

    d_context = sum_row(
        lax.dot_general(grad_all, w_out, (((1,), (1,)), ((), ())), preferred_element_type=F32)
    )
    qkv = sum_row(jnp.dot(normed_all, w_qkv, preferred_element_type=F32))
    context, d_qkv, terms = attention(block_starts(block), qkv, d_context, u)

    partial, gain_part = input_partial(features, d_qkv, w_qkv, normed_all, gain[None], terms)
    total = scatter_col(partial)
    gain_grad = jnp.sum(exchange(gain_part[0], "col"), axis=0)
    tn = (((0,), (0,)), ((), ()))
    grad_wout = lax.dot_general(context, grad_all, tn, preferred_element_type=F32).astype(BF16)
    grad_wqkv = lax.dot_general(normed_all, d_qkv, tn, preferred_element_type=F32).astype(BF16)
    return (total * rstd[:, None]).astype(BF16), gain_grad, grad_wqkv, grad_wout


def solution(mesh):
    in_specs = (
        P(("dp", "col"), "row"),
        P("row"),
        P("row", "col"),
        P("col", "row"),
        P(("dp", "col"), "row"),
    )
    out_specs = (
        P(("dp", "col"), "row"),
        P(("dp", "row")),
        P(("dp", "row"), "col"),
        P(("dp", "col"), "row"),
    )
    return jax.shard_map(shards, mesh=mesh, in_specs=in_specs, out_specs=out_specs, check_vma=False)
```

```python
import functools
import math

import jax
import jax.numpy as jnp
from jax import lax
from jax.experimental import pallas as pl
from jax.experimental.pallas import tpu as pltpu
from jax.sharding import PartitionSpec as P

HS = 128
EPS = 1e-05
F32 = jnp.float32
BF16 = jnp.bfloat16
QB = 256
VMEM_LIMIT = 48 * 1024 * 1024


def to_row(v, dx, dy):
    return lax.ppermute(v, "row", [(r, ((r // 2 + dx) % 4) * 2 + ((r % 2) ^ dy)) for r in range(8)])


def to_core(v):
    return lax.ppermute(v, "col", [(c, c ^ 1) for c in range(16)])


def onward(v, hops=1):
    return lax.ppermute(v, "col", [(c, ((c // 2 + hops - 2 * hops * (c % 2)) % 8) * 2 + c % 2) for c in range(16)])


def after(v, *others):
    return lax.optimization_barrier((v, *others))[0]


ORDER = [(0, 0), (0, 1), (-4, 0), (-4, 1)]
for d in (1, 2, 3):
    ORDER += [(-d, 0), (-d, 1), (d, 1), (d, 0)]


def gathered(own, swap, one, two, three, far):
    return [own, swap, far, to_core(far), one, to_core(one), two, to_core(two), three, to_core(three)]


def exchange(v, axis):
    n = lax.axis_size(axis)
    return lax.all_to_all(jnp.broadcast_to(v[None], (n, *v.shape)), axis, 0, 0)


def f32_sum(first, *others):
    total = first.astype(F32)
    for other in others:
        total = total + other.astype(F32)
    return total


class XFirst:
    kind = "x"

    def __init__(self, parts):
        self.terms = [parts[0]] + [to_row(parts[d], d, 0) for d in (1, 2, 3)]

    def step1(self, token):
        self.terms[0] = after(self.terms[0], token)
        sent = f32_sum(*self.terms).astype(BF16)
        self.terms.append(to_row(sent, 0, 1))
        return sent

    def step2(self, token):
        self.terms[0] = after(self.terms[0], token)
        mine = f32_sum(*self.terms).astype(BF16)
        self.pieces = [mine] + [to_row(mine, -d, 0) for d in (1, 2, 3)]
        return mine


class YFirst:
    kind = "y"

    def __init__(self, parts):
        self.keep, self.come = parts[0], to_row(parts[1], 0, 1)

    def step1(self, token):
        kept = f32_sum(after(self.keep, token), self.come)
        rows = kept.shape[0] // 4
        sent = [kept[d * rows : (d + 1) * rows].astype(BF16) for d in range(4)]
        self.terms = [kept[:rows]] + [to_row(sent[d], d, 0) for d in (1, 2, 3)]
        return sent[3]

    def step2(self, token):
        self.mine = f32_sum(after(self.terms[0], token), *self.terms[1:]).astype(BF16)
        self.others = [to_row(self.mine, -d, 0) for d in (1, 2, 3)]
        return self.mine

    def step3(self, token):
        half = jnp.concatenate([after(self.mine, token), *self.others], axis=0)
        self.pieces = [half, to_row(half, 0, 1)]
        return half


def places(block):
    r, c = lax.axis_index("row"), lax.axis_index("col")
    z, core = c // 2, c % 2
    way = 1 - 2 * core
    steps = jnp.array([d for d, _ in ORDER], jnp.int32)
    other = jnp.array([o for _, o in ORDER], jnp.int32)
    starts = (((z + way * steps) % 8) * 2 + (core + other) % 2) * block
    return jnp.concatenate([starts, jnp.stack([r // 2, r % 2])]).astype(jnp.int32)


def row_parts(kind, place, partial, outs):
    x, y = place[16], place[17]
    if kind == "x":
        for d, out in enumerate(outs):
            rows = out.shape[0]
            out[...] = partial[pl.ds(pl.multiple_of(((x + d) % 4) * rows, rows), rows), :]
    else:
        for half, out in zip((y, 1 - y), outs):
            rows = out.shape[0] // 4
            for d in range(4):
                start = pl.multiple_of((half * 4 + (x + d) % 4) * rows, rows)
                out[d * rows : (d + 1) * rows, :] = partial[pl.ds(start, rows), :]


def part_shapes(kind, tokens, width):
    count = 4 if kind == "x" else 2
    return [jax.ShapeDtypeStruct((tokens // count, width), BF16)] * count


def whole(v):
    return pl.BlockSpec(v.shape, lambda i, place: (0,) * len(v.shape))


def one_step(kernel, name, place, inputs, in_specs, outs, flops, scratch=()):
    moved = sum(math.prod(v.shape) * v.dtype.itemsize for v in [*inputs, *outs])
    return pl.pallas_call(
        kernel,
        grid_spec=pltpu.PrefetchScalarGridSpec(
            num_scalar_prefetch=1,
            grid=(1,),
            in_specs=in_specs,
            out_specs=[whole(v) for v in outs],
            scratch_shapes=list(scratch),
        ),
        out_shape=outs,
        compiler_params=pltpu.CompilerParams(vmem_limit_bytes=VMEM_LIMIT),
        cost_estimate=pl.CostEstimate(flops=flops, bytes_accessed=moved, transcendentals=0),
        name=name,
    )(place, *inputs)


def context_kernel(kind, place, *refs):
    *pieces, w_ref, all_ref = refs[:12]
    outs, partial = refs[12:-1], refs[-1]
    nt = (((1,), (1,)), ((), ()))
    at = 0
    for piece in pieces:
        all_ref[at : at + piece.shape[0], :] = piece[...]
        at += piece.shape[0]
    partial[...] = lax.dot_general(all_ref[...], w_ref[...], nt, preferred_element_type=F32).astype(BF16)
    row_parts(kind, place, partial, outs)


def context_partial(kind, place, pieces, w_out):
    tokens, here = sum(p.shape[0] for p in pieces), pieces[0].shape[1]
    width = w_out.shape[0]
    outs = [jax.ShapeDtypeStruct((tokens, here), BF16), *part_shapes(kind, tokens, width)]
    inputs = [*pieces, w_out]
    return one_step(
        functools.partial(context_kernel, kind), "context_partial", place, inputs, [whole(v) for v in inputs], outs,
        2 * tokens * here * width, [pltpu.VMEM((tokens, width), BF16)],
    )


def projection_kernel(kinds, split, place, *refs):
    *pieces, stat_ref, gain_ref, w_ref, all_ref = refs[:14]
    outs, first, second = refs[14:-2], refs[-2], refs[-1]
    block = pieces[0].shape[0]
    at = 0
    for piece in pieces:
        for i in range(piece.shape[0] // block):
            stats = stat_ref[at : at + block, :]
            x = piece[i * block : (i + 1) * block, :].astype(F32)
            all_ref[at : at + block, :] = ((x - stats[:, 0:1]) * stats[:, 1:2] * gain_ref[...]).astype(BF16)
            at += block
    first[...] = jnp.dot(all_ref[...], w_ref[:, :split], preferred_element_type=F32).astype(BF16)
    row_parts(kinds[0], place, first, outs[:4])
    second[...] = jnp.dot(all_ref[...], w_ref[:, split:], preferred_element_type=F32).astype(BF16)
    row_parts(kinds[1], place, second, outs[4:])


def projection(kinds, split, place, pieces, stats, gain, w_qkv):
    tokens, here = sum(p.shape[0] for p in pieces), pieces[0].shape[1]
    width = w_qkv.shape[1]
    outs = [jax.ShapeDtypeStruct((tokens, here), BF16), *part_shapes(kinds[0], tokens, split)]
    outs += part_shapes(kinds[1], tokens, width - split)
    inputs = [*pieces, stats, gain, w_qkv]
    return one_step(
        functools.partial(projection_kernel, kinds, split), "projection", place, inputs, [whole(v) for v in inputs], outs,
        2 * tokens * here * width, [pltpu.VMEM((tokens, split), BF16), pltpu.VMEM((tokens, width - split), BF16)],
    )


def unpack(kind, place, pieces, to_ref, at):
    x, y = place[16], place[17]
    block = to_ref.shape[0] // 16
    for b in range(16):
        if kind == "x":
            piece, i = pieces[b // 4], b % 4
            of = (x + b // 4) % 4 * 4 + i
        else:
            piece, i = pieces[b // 8], b % 8
            of = (y if b < 8 else 1 - y) * 8 + (x + i // 2) % 4 * 2 + i % 2
        to = pl.ds(pl.multiple_of(place[of], block), block)
        to_ref[to, at : at + HS] = piece[i * block : (i + 1) * block, :]


def attention_kernel(units, head, place, *refs):
    ctx_ref, dqkv_ref, term_ref, qkv, dout, dkv, dall, ctx_s = refs[-8:]
    tokens = qkv.shape[0]
    block = tokens // 16
    scale = 1.0 / math.sqrt(HS)
    nt = (((1,), (1,)), ((), ()))
    for i, (kind, count) in enumerate(units):
        unpack(kind, place, refs[:count], qkv if i < 3 else dout, i * HS if i < 3 else 0)
        refs = refs[count:]
    u_ref, *before = refs[: 4 if head else 1]

    dkv[...] = jnp.zeros_like(dkv)
    k_t = qkv[:, HS : 2 * HS].T
    v_t = qkv[:, 2 * HS : 3 * HS].T
    key_at = lax.broadcasted_iota(jnp.int32, (QB, QB), 0)
    query_at = lax.broadcasted_iota(jnp.int32, (QB, QB), 1)
    for i in range(tokens // QB):
        lo, hi = i * QB, (i + 1) * QB
        query = qkv[lo:hi, :HS]
        grad = dout[lo:hi, :]
        keys = qkv[:hi, HS : 2 * HS]
        values = qkv[:hi, 2 * HS : 3 * HS]
        s = lax.dot_general(keys, query, nt, preferred_element_type=F32) * (scale * math.log2(math.e))
        last = jnp.where(key_at <= query_at, s[lo:hi], -jnp.inf)
        s = jnp.concatenate([s[:lo], last], axis=0) if i else last
        powers = jnp.exp2(s - jnp.max(s, axis=0, keepdims=True))
        probs = powers * (1.0 / jnp.sum(powers, axis=0, keepdims=True))
        probs_b = probs.astype(BF16)
        d_probs = lax.dot_general(values, grad, nt, preferred_element_type=F32)
        delta = jnp.sum(probs * d_probs, axis=0, keepdims=True)
        d_scores = (probs * (d_probs - delta) * scale).astype(BF16)
        ctx_s[lo:hi, :] = jnp.dot(v_t[:, :hi], probs_b, preferred_element_type=F32).T.astype(BF16)
        dall[lo:hi, :HS] = jnp.dot(k_t[:, :hi], d_scores, preferred_element_type=F32).T.astype(BF16)
        dkv[:hi, :HS] += jnp.dot(d_scores, query, preferred_element_type=F32)
        dkv[:hi, HS:] += jnp.dot(probs_b, grad, preferred_element_type=F32)
    dall[:, HS:] = dkv[...].astype(BF16)

    for b in range(16):
        src = pl.ds(pl.multiple_of(place[b], block), block)
        to = slice(b * block, (b + 1) * block)
        piece = dall[src, :]
        dqkv_ref[to, :] = piece
        ctx_ref[to, :] = ctx_s[src, :]
        wide = piece.astype(F32)
        first = jnp.sum(wide * u_ref[...], axis=1, keepdims=True)
        second = jnp.sum(wide * qkv[src, :].astype(F32), axis=1, keepdims=True)
        lane = lax.broadcasted_iota(jnp.int32, (block, HS), 1)
        both = jnp.where(lane == 0, first, jnp.where(lane == 1, second, 0.0))
        term_ref[to, :] = both if head == 0 else before[2][to, :] + both


def attention(head, place, first, second, grads, u, before):
    tokens = sum(p.shape[0] for p in first.pieces)
    heads = u.shape[1] // (3 * HS)
    split = first.pieces[0].shape[1] // HS
    shapes = [
        jax.ShapeDtypeStruct((tokens, heads * HS), BF16),
        jax.ShapeDtypeStruct((tokens, heads * 3 * HS), BF16),
        jax.ShapeDtypeStruct((tokens, HS), F32),
    ]

    def columns(rows, cols, at):
        return pl.BlockSpec((rows, cols), lambda i, place: (0, at))

    units, inputs, specs = [], [], []
    for unit, at in [(first, c) if c < split else (second, c - split) for c in range(3 * head, 3 * head + 3)] + [(grads, head)]:
        units.append((unit.kind, len(unit.pieces)))
        inputs += unit.pieces
        specs += [columns(p.shape[0], HS, at) for p in unit.pieces]
    terms = columns(tokens, HS, 0)
    anywhere = pl.BlockSpec(memory_space=pl.ANY)
    return pl.pallas_call(
        functools.partial(attention_kernel, units, head),
        grid_spec=pltpu.PrefetchScalarGridSpec(
            num_scalar_prefetch=1,
            grid=(1,),
            in_specs=specs + [columns(1, 3 * HS, head)] + ([anywhere, anywhere, terms] if head else []),
            out_specs=[columns(tokens, HS, head), columns(tokens, 3 * HS, head), terms],
            scratch_shapes=[
                pltpu.VMEM((tokens, 3 * HS), BF16),
                pltpu.VMEM((tokens, HS), BF16),
                pltpu.VMEM((tokens, 2 * HS), F32),
                pltpu.VMEM((tokens, 3 * HS), BF16),
                pltpu.VMEM((tokens, HS), BF16),
            ],
        ),
        out_shape=shapes,
        input_output_aliases={len(inputs) + 2 + i: i for i in range(2)} if head else {},
        compiler_params=pltpu.CompilerParams(vmem_limit_bytes=VMEM_LIMIT),
        cost_estimate=pl.CostEstimate(
            flops=tokens * tokens * HS * 12 * 5 // 4,
            bytes_accessed=tokens * HS * 20,
            transcendentals=tokens * tokens * 5 // 8,
        ),
        name="attention",
    )(place, *inputs, u, *(before or []))


def input_kernel(features, dqkv_ref, w_ref, normed_ref, gain_ref, term_ref, keep_ref, send_ref, gain_grad_ref):
    nt = (((1,), (1,)), ((), ()))
    d_normed = lax.dot_general(dqkv_ref[...], w_ref[...], nt, preferred_element_type=F32)
    gain = gain_ref[...]
    inverse = 1.0 / gain
    normed = normed_ref[...].astype(F32)
    first = term_ref[:, 0:1] * (1.0 / features)
    second = term_ref[:, 1:2] * (1.0 / features)
    out = (d_normed * gain - first - normed * inverse * second).astype(BF16)
    part = jnp.sum(d_normed * normed, axis=0, keepdims=True) * inverse
    step = pl.program_id(0)
    quarter = out.shape[0] // 4

    @pl.when(step == 0)
    def _():
        keep_ref[:quarter, :] = out[:quarter]
        keep_ref[quarter:, :] = out[3 * quarter :]
        send_ref[...] = out[quarter : 3 * quarter]
        gain_grad_ref[...] = part

    @pl.when(step > 0)
    def _():
        keep_ref[...] = out[2 * quarter :]
        send_ref[...] = out[: 2 * quarter]
        gain_grad_ref[...] += part


def input_partial(features, d_qkv, w_qkv, normed, gain, terms, at, parts):
    tokens, width = d_qkv.shape
    here = w_qkv.shape[0] // parts
    rows = tokens // 4
    half = pl.BlockSpec((rows // 2, here), lambda i: (i, 0))
    return pl.pallas_call(
        functools.partial(input_kernel, features),
        grid=(4,),
        in_specs=[
            pl.BlockSpec((rows, width), lambda i: (i, 0)),
            pl.BlockSpec((here, width), lambda i: (at, 0)),
            pl.BlockSpec((rows, here), lambda i: (i, at)),
            pl.BlockSpec((1, here), lambda i: (0, at)),
            pl.BlockSpec((rows, HS), lambda i: (i, 0)),
        ],
        out_specs=[half, half, pl.BlockSpec((1, here), lambda i: (0, 0))],
        out_shape=[
            jax.ShapeDtypeStruct((tokens // 2, here), BF16),
            jax.ShapeDtypeStruct((tokens // 2, here), BF16),
            jax.ShapeDtypeStruct((1, here), F32),
        ],
        compiler_params=pltpu.CompilerParams(vmem_limit_bytes=VMEM_LIMIT),
        cost_estimate=pl.CostEstimate(
            flops=2 * tokens * width * here,
            bytes_accessed=2 * (tokens * width + width * here + 2 * tokens * here),
            transcendentals=0,
        ),
        name="input_partial",
    )(d_qkv, w_qkv, normed, gain, terms)


def scatter_start(keep, send):
    block = keep.shape[0] // 8
    kept = f32_sum(keep, to_core(send))
    own, far, one, two, three = jnp.split(kept, [block, 2 * block, 4 * block, 6 * block], axis=0)
    far = far.astype(BF16)
    return own, one, two, onward(far, 2), onward(three.astype(BF16)), far


def scatter_middle(own, one, two, far_come, three_come):
    block = own.shape[0]
    two = two + three_come.astype(F32)
    two = jnp.concatenate([two[:block] + far_come.astype(F32), two[block:]], axis=0).astype(BF16)
    return own, onward(two, 2), onward(one.astype(BF16)), two


def scatter_end(own, two_come, one_come):
    block = own.shape[0]
    come = f32_sum(two_come, one_come)
    return own + come[block:], to_core(come[:block].astype(BF16))


def shards(layer_input, gain, w_qkv, w_out, out_grad):
    block, here = layer_input.shape
    features = here * lax.axis_size("row")
    place = places(block)

    swap = to_core(layer_input)
    pair = jnp.concatenate([layer_input, swap], axis=0)

    x = layer_input.astype(F32)
    mean_here = jnp.sum(x, axis=1) / here
    apart = x - mean_here[:, None]
    squares_here = jnp.sum(apart * apart, axis=1)
    u_here = jnp.sum(w_qkv.astype(F32) * gain[:, None], axis=0)
    told_here = after(jnp.broadcast_to(jnp.concatenate([mean_here, squares_here, u_here])[None], (8, 2*block+u_here.shape[0])), pair)
    one, told = lax.optimization_barrier((onward(pair), lax.all_to_all(told_here, "row", 0, 0)))
    means, squares = told[:, :block], told[:, block : 2 * block]
    mean = jnp.mean(means, axis=0)
    variance = (jnp.sum(squares, axis=0) + here * jnp.sum((means - mean) ** 2, axis=0)) / features
    rstd = lax.rsqrt(variance + EPS)
    u = jnp.sum(told[:, 2 * block :], axis=0)[None]
    own_stats = jnp.concatenate([mean, rstd])[None]
    pair_stats = jnp.concatenate([own_stats, to_core(own_stats)], axis=0)
    stats = [onward(pair_stats[:1], 4)] + [onward(pair_stats, d) for d in (1, 2, 3)]
    others = to_core(jnp.concatenate(stats, axis=0))
    rows = [pair_stats, stats[0], others[:1]]
    for d in (1, 2, 3):
        rows += [stats[d], others[2 * d - 1 : 2 * d + 1]]
    stats = jnp.concatenate(rows, axis=0).reshape(16, 2, block)
    stats = jnp.transpose(stats, (0, 2, 1)).reshape(16 * block, 2)

    two = onward(one)
    three, far = onward(two), onward(two[:block], 2)
    pieces = gathered(layer_input, swap, one, two, three, far)
    grad_own = after(out_grad, two)
    grad_swap = to_core(grad_own)
    grad_one = onward(jnp.concatenate([grad_own, grad_swap], axis=0))
    grad_two = onward(after(grad_one, three, far))
    grad_three, grad_far = onward(grad_two), onward(grad_two[:block], 2)
    grad_pieces = gathered(out_grad, grad_swap, grad_one, grad_two, grad_three, grad_far)

    split = 5 * HS
    normed, *parts = projection("xy", split, place, pieces, stats, gain[None], w_qkv)
    first, second = XFirst(parts[:4]), YFirst(parts[4:])
    token = first.step1(gain)
    token = second.step1(token)
    grad_all, *parts = context_partial("y", after(place, token), grad_pieces, w_out)
    grads = YFirst(parts)
    token = first.step2(parts[0])
    token = second.step2(token)
    token = grads.step1(token)
    token = second.step3(token)
    token = grads.step2(token)
    token = grads.step3(token)
    done = None
    for head in range(w_qkv.shape[1] // (3 * HS)):
        done = attention(head, place, first, second, grads, u, done)
    context, d_qkv, terms = done

    halves, gain_parts = [], []
    parts = 2
    for at in range(parts):
        keep, send, gain_part = input_partial(features, d_qkv, w_qkv, normed, gain[None], terms, at, parts)
        halves.append(scatter_start(keep, send))
        gain_parts.append(gain_part[0])
    tn = (((0,), (0,)), ((), ()))
    grad_wqkv = lax.dot_general(after(normed, halves[0][-1], halves[1][-1]), d_qkv, tn, preferred_element_type=F32).astype(BF16)
    halves = [scatter_middle(*half[:-1]) for half in halves]
    grad_wout = lax.dot_general(after(context, halves[0][-1], halves[1][-1]), grad_all, tn, preferred_element_type=F32).astype(BF16)
    gain_grad = jnp.sum(exchange(after(jnp.concatenate(gain_parts), halves[0][-1], halves[1][-1]), "col"), axis=0)
    halves = [scatter_end(*half[:-1]) for half in halves]
    total = jnp.concatenate([f32_sum(*half) for half in halves], axis=1)
    return (total * rstd[:, None]).astype(BF16), gain_grad, grad_wqkv, grad_wout


def solution(mesh):
    in_specs = (
        P(("dp", "col"), "row"),
        P("row"),
        P("row", "col"),
        P("col", "row"),
        P(("dp", "col"), "row"),
    )
    out_specs = (
        P(("dp", "col"), "row"),
        P(("dp", "row")),
        P(("dp", "row"), "col"),
        P(("dp", "col"), "row"),
    )
    return jax.shard_map(shards, mesh=mesh, in_specs=in_specs, out_specs=out_specs, check_vma=False)
```

```python
import functools
import math

import jax
import jax.numpy as jnp
from jax import lax
from jax.experimental import pallas as pl
from jax.experimental.pallas import tpu as pltpu
from jax.sharding import PartitionSpec as P

HS = 128
EPS = 1e-05
F32 = jnp.float32
BF16 = jnp.bfloat16
QB = 256
VMEM_LIMIT = 48 * 1024 * 1024


def to_row(v, dx, dy):
    return lax.ppermute(v, "row", [(r, ((r // 2 + dx) % 4) * 2 + ((r % 2) ^ dy)) for r in range(8)])


def to_core(v):
    return lax.ppermute(v, "col", [(c, c ^ 1) for c in range(16)])


def onward(v, hops=1):
    return lax.ppermute(v, "col", [(c, ((c // 2 + hops - 2 * hops * (c % 2)) % 8) * 2 + c % 2) for c in range(16)])


def after(v, *others):
    return lax.optimization_barrier((v, *others))[0]


def together(*groups):
    return lax.optimization_barrier(groups)


ORDER = [(0, 0), (-4, 1), (1, 1), (1, 0), (2, 1), (2, 0), (3, 1), (3, 0)]
ORDER += [(0, 1), (-4, 0), (-1, 0), (-1, 1), (-2, 0), (-2, 1), (-3, 0), (-3, 1)]


def gathered(own, swap, one, two, three, far):
    return [own] + [to_core(v) for v in (far, one, two, three)] + [swap, far, one, two, three]


def exchange(v, axis):
    n = lax.axis_size(axis)
    return lax.all_to_all(jnp.broadcast_to(v[None], (n, *v.shape)), axis, 0, 0)


def f32_sum(first, *others):
    total = first.astype(F32)
    for other in others:
        total = total + other.astype(F32)
    return total


class XFirst:
    kind = "x"

    def __init__(self, parts):
        self.terms = [parts[0]] + [to_row(parts[d], d, 0) for d in (1, 2, 3)]

    def step1(self, token):
        self.terms[0] = after(self.terms[0], token)
        sent = f32_sum(*self.terms).astype(BF16)
        self.terms.append(to_row(sent, 0, 1))
        return sent

    def step2(self, token):
        self.terms[0] = after(self.terms[0], token)
        mine = f32_sum(*self.terms).astype(BF16)
        self.pieces = [mine] + [to_row(mine, -d, 0) for d in (1, 2, 3)]
        return mine


class YFirst:
    kind = "y"

    def __init__(self, parts):
        self.keep, self.come = parts[0], to_row(parts[1], 0, 1)

    def step1(self, token):
        kept = f32_sum(after(self.keep, token), self.come)
        rows = kept.shape[0] // 4
        sent = [kept[d * rows : (d + 1) * rows].astype(BF16) for d in range(4)]
        self.terms = [kept[:rows]] + [to_row(sent[d], d, 0) for d in (1, 2, 3)]
        return sent[3]

    def step2(self, token):
        self.mine = f32_sum(after(self.terms[0], token), *self.terms[1:]).astype(BF16)
        self.others = [to_row(self.mine, -d, 0) for d in (1, 2, 3)]
        return self.mine

    def step3(self, token):
        half = jnp.concatenate([after(self.mine, token), *self.others], axis=0)
        self.pieces = [half, to_row(half, 0, 1)]
        return half


def places(block):
    r, c = lax.axis_index("row"), lax.axis_index("col")
    z, core = c // 2, c % 2
    way = 1 - 2 * core
    steps = jnp.array([d for d, _ in ORDER], jnp.int32)
    other = jnp.array([o for _, o in ORDER], jnp.int32)
    starts = (((z + way * steps) % 8) * 2 + (core + other) % 2) * block
    return jnp.concatenate([starts, jnp.stack([r // 2, r % 2])]).astype(jnp.int32)


def row_parts(kind, place, partial, outs):
    x, y = place[16], place[17]
    if kind == "x":
        for d, out in enumerate(outs):
            rows = out.shape[0]
            out[...] = partial[pl.ds(pl.multiple_of(((x + d) % 4) * rows, rows), rows), :]
    else:
        for half, out in zip((y, 1 - y), outs):
            rows = out.shape[0] // 4
            for d in range(4):
                start = pl.multiple_of((half * 4 + (x + d) % 4) * rows, rows)
                out[d * rows : (d + 1) * rows, :] = partial[pl.ds(start, rows), :]


def part_shapes(kind, tokens, width):
    count = 4 if kind == "x" else 2
    return [jax.ShapeDtypeStruct((tokens // count, width), BF16)] * count


def whole(v):
    return pl.BlockSpec(v.shape, lambda i, place: (0,) * len(v.shape))


def one_step(kernel, name, place, inputs, in_specs, outs, flops, scratch=()):
    moved = sum(math.prod(v.shape) * v.dtype.itemsize for v in [*inputs, *outs])
    return pl.pallas_call(
        kernel,
        grid_spec=pltpu.PrefetchScalarGridSpec(
            num_scalar_prefetch=1,
            grid=(1,),
            in_specs=in_specs,
            out_specs=[whole(v) for v in outs],
            scratch_shapes=list(scratch),
        ),
        out_shape=outs,
        compiler_params=pltpu.CompilerParams(vmem_limit_bytes=VMEM_LIMIT),
        cost_estimate=pl.CostEstimate(flops=flops, bytes_accessed=moved, transcendentals=0),
        name=name,
    )(place, *inputs)


def context_kernel(kind, place, *refs):
    *pieces, w_ref, all_ref = refs[:12]
    outs, partial = refs[12:-1], refs[-1]
    nt = (((1,), (1,)), ((), ()))
    at = 0
    for piece in pieces:
        all_ref[at : at + piece.shape[0], :] = piece[...]
        at += piece.shape[0]
    partial[...] = lax.dot_general(all_ref[...], w_ref[...], nt, preferred_element_type=F32).astype(BF16)
    row_parts(kind, place, partial, outs)


def context_partial(kind, place, pieces, w_out):
    tokens, here = sum(p.shape[0] for p in pieces), pieces[0].shape[1]
    width = w_out.shape[0]
    outs = [jax.ShapeDtypeStruct((tokens, here), BF16), *part_shapes(kind, tokens, width)]
    inputs = [*pieces, w_out]
    return one_step(
        functools.partial(context_kernel, kind), "context_partial", place, inputs, [whole(v) for v in inputs], outs,
        2 * tokens * here * width, [pltpu.VMEM((tokens, width), BF16)],
    )


def projection_kernel(kinds, split, place, *refs):
    *pieces, stat_ref, gain_ref, w_ref, all_ref = refs[:14]
    outs, first, second = refs[14:-2], refs[-2], refs[-1]
    block = pieces[0].shape[0]
    at = 0
    for piece in pieces:
        for i in range(piece.shape[0] // block):
            stats = stat_ref[at : at + block, :]
            x = piece[i * block : (i + 1) * block, :].astype(F32)
            all_ref[at : at + block, :] = ((x - stats[:, 0:1]) * stats[:, 1:2] * gain_ref[...]).astype(BF16)
            at += block
    first[...] = jnp.dot(all_ref[...], w_ref[:, :split], preferred_element_type=F32).astype(BF16)
    row_parts(kinds[0], place, first, outs[:4])
    second[...] = jnp.dot(all_ref[...], w_ref[:, split:], preferred_element_type=F32).astype(BF16)
    row_parts(kinds[1], place, second, outs[4:])


def projection(kinds, split, place, pieces, stats, gain, w_qkv):
    tokens, here = sum(p.shape[0] for p in pieces), pieces[0].shape[1]
    width = w_qkv.shape[1]
    outs = [jax.ShapeDtypeStruct((tokens, here), BF16), *part_shapes(kinds[0], tokens, split)]
    outs += part_shapes(kinds[1], tokens, width - split)
    inputs = [*pieces, stats, gain, w_qkv]
    return one_step(
        functools.partial(projection_kernel, kinds, split), "projection", place, inputs, [whole(v) for v in inputs], outs,
        2 * tokens * here * width, [pltpu.VMEM((tokens, split), BF16), pltpu.VMEM((tokens, width - split), BF16)],
    )


def unpack(kind, place, pieces, column, to_ref, at):
    x, y = place[16], place[17]
    block = to_ref.shape[0] // 16
    for b in range(16):
        if kind == "x":
            piece, i = pieces[b // 4], b % 4
            of = (x + b // 4) % 4 * 4 + i
        else:
            piece, i = pieces[b // 8], b % 8
            of = (y if b < 8 else 1 - y) * 8 + (x + i // 2) % 4 * 2 + i % 2
        to = pl.ds(pl.multiple_of(place[of], block), block)
        to_ref[to, at : at + HS] = piece[i * block : (i + 1) * block, column : column + HS]


def attention_kernel(heads, kinds, counts, place, *refs):
    head = pl.program_id(0)
    u_ref, ctx_ref, dqkv_ref, term_ref, qkv, dout, dkv, dall, ctx_s = refs[-9:]
    units = refs[: counts[0]], refs[counts[0] : sum(counts)]
    split = units[0][0].shape[1]
    tokens = qkv.shape[0]
    block = tokens // 16
    scale = 1.0 / math.sqrt(HS)
    nt = (((1,), (1,)), ((), ()))
    for h in range(heads):

        @pl.when(head == h)
        def _():
            for i in range(3):
                at = (3 * h + i) * HS
                unit, at = (0, at) if at < split else (1, at - split)
                unpack(kinds[unit], place, units[unit], at, qkv, i * HS)

    unpack(kinds[2], place, refs[sum(counts) : -9], 0, dout, 0)

    dkv[...] = jnp.zeros_like(dkv)
    k_t = qkv[:, HS : 2 * HS].T
    v_t = qkv[:, 2 * HS : 3 * HS].T
    key_at = lax.broadcasted_iota(jnp.int32, (QB, QB), 0)
    query_at = lax.broadcasted_iota(jnp.int32, (QB, QB), 1)
    for i in range(tokens // QB):
        lo, hi = i * QB, (i + 1) * QB
        query = qkv[lo:hi, :HS]
        grad = dout[lo:hi, :]
        keys = qkv[:hi, HS : 2 * HS]
        values = qkv[:hi, 2 * HS : 3 * HS]
        s = lax.dot_general(keys, query, nt, preferred_element_type=F32) * (scale * math.log2(math.e))
        last = jnp.where(key_at <= query_at, s[lo:hi], -jnp.inf)
        s = jnp.concatenate([s[:lo], last], axis=0) if i else last
        powers = jnp.exp2(s - jnp.max(s, axis=0, keepdims=True))
        probs = powers * (1.0 / jnp.sum(powers, axis=0, keepdims=True))
        probs_b = probs.astype(BF16)
        d_probs = lax.dot_general(values, grad, nt, preferred_element_type=F32)
        delta = jnp.sum(probs * d_probs, axis=0, keepdims=True)
        d_scores = (probs * (d_probs - delta) * scale).astype(BF16)
        ctx_s[lo:hi, :] = jnp.dot(v_t[:, :hi], probs_b, preferred_element_type=F32).T.astype(BF16)
        dall[lo:hi, :HS] = jnp.dot(k_t[:, :hi], d_scores, preferred_element_type=F32).T.astype(BF16)
        dkv[:hi, :HS] += jnp.dot(d_scores, query, preferred_element_type=F32)
        dkv[:hi, HS:] += jnp.dot(probs_b, grad, preferred_element_type=F32)
    dall[:, HS:] = dkv[...].astype(BF16)

    for b in range(16):
        src = pl.ds(pl.multiple_of(place[b], block), block)
        to = slice(b * block, (b + 1) * block)
        piece = dall[src, :]
        dqkv_ref[to, :] = piece
        ctx_ref[to, :] = ctx_s[src, :]
        wide = piece.astype(F32)
        first = jnp.sum(wide * u_ref[...], axis=1, keepdims=True)
        second = jnp.sum(wide * qkv[src, :].astype(F32), axis=1, keepdims=True)
        lane = lax.broadcasted_iota(jnp.int32, (block, HS), 1)
        both = jnp.where(lane == 0, first, jnp.where(lane == 1, second, 0.0))

        @pl.when(head == 0)
        def _():
            term_ref[to, :] = both

        @pl.when(head > 0)
        def _():
            term_ref[to, :] += both


def attention(place, first, second, grads, u):
    tokens = sum(p.shape[0] for p in grads.pieces)
    heads = u.shape[1] // (3 * HS)
    pieces = first.pieces + second.pieces
    shapes = [
        jax.ShapeDtypeStruct((tokens, heads * HS), BF16),
        jax.ShapeDtypeStruct((tokens, heads * 3 * HS), BF16),
        jax.ShapeDtypeStruct((tokens, HS), F32),
    ]

    def by_head(rows, cols):
        return pl.BlockSpec((rows, cols), lambda h, place: (0, h))

    return pl.pallas_call(
        functools.partial(
            attention_kernel, heads, (first.kind, second.kind, grads.kind), (len(first.pieces), len(second.pieces))
        ),
        grid_spec=pltpu.PrefetchScalarGridSpec(
            num_scalar_prefetch=1,
            grid=(heads,),
            in_specs=[whole(p) for p in pieces] + [by_head(p.shape[0], HS) for p in grads.pieces] + [by_head(1, 3 * HS)],
            out_specs=[by_head(tokens, HS), by_head(tokens, 3 * HS), pl.BlockSpec((tokens, HS), lambda h, place: (0, 0))],
            scratch_shapes=[
                pltpu.VMEM((tokens, 3 * HS), BF16),
                pltpu.VMEM((tokens, HS), BF16),
                pltpu.VMEM((tokens, 2 * HS), F32),
                pltpu.VMEM((tokens, 3 * HS), BF16),
                pltpu.VMEM((tokens, HS), BF16),
            ],
        ),
        out_shape=shapes,
        compiler_params=pltpu.CompilerParams(vmem_limit_bytes=VMEM_LIMIT),
        cost_estimate=pl.CostEstimate(
            flops=heads * tokens * tokens * HS * 12 * 5 // 8,
            bytes_accessed=heads * tokens * HS * 20,
            transcendentals=heads * tokens * tokens * 5 // 8,
        ),
        name="attention",
    )(place, *pieces, *grads.pieces, u)


def scatter_start(keep, come):
    block = keep.shape[0] // 8
    kept = f32_sum(keep, come)
    own, far, one, two, three = jnp.split(kept, [block, 2 * block, 4 * block, 6 * block], axis=0)
    return own, one, two, three.astype(BF16), far.astype(BF16)


def scatter_middle(own, one, two, far_come, three_come):
    block = own.shape[0]
    two = two + three_come.astype(F32)
    two = jnp.concatenate([two[:block] + far_come.astype(F32), two[block:]], axis=0)
    return own, one.astype(BF16), two.astype(BF16)


def scatter_end(own, two_come, one_come):
    block = own.shape[0]
    come = f32_sum(two_come, one_come)
    return own + come[block:], to_core(come[:block].astype(BF16))


def shards(layer_input, gain, w_qkv, w_out, out_grad):
    block, here = layer_input.shape
    features = here * lax.axis_size("row")
    place = places(block)

    swap = to_core(layer_input)
    pair = jnp.concatenate([layer_input, swap], axis=0)

    x = layer_input.astype(F32)
    mean_here = jnp.sum(x, axis=1) / here
    apart = x - mean_here[:, None]
    squares_here = jnp.sum(apart * apart, axis=1)
    u_here = jnp.sum(w_qkv.astype(F32) * gain[:, None], axis=0)
    told_here = after(jnp.broadcast_to(jnp.concatenate([mean_here, squares_here, u_here])[None], (8, 2*block+u_here.shape[0])), pair)
    one, told = lax.optimization_barrier((onward(pair), lax.all_to_all(told_here, "row", 0, 0)))
    means, squares = told[:, :block], told[:, block : 2 * block]
    mean = jnp.mean(means, axis=0)
    variance = (jnp.sum(squares, axis=0) + here * jnp.sum((means - mean) ** 2, axis=0)) / features
    rstd = lax.rsqrt(variance + EPS)
    u = jnp.sum(told[:, 2 * block :], axis=0)[None]
    own_stats = jnp.concatenate([mean, rstd])[None]
    pair_stats = jnp.concatenate([own_stats, to_core(own_stats)], axis=0)
    stats = [onward(pair_stats[:1], 4)] + [onward(pair_stats, d) for d in (1, 2, 3)]
    others = to_core(jnp.concatenate(stats, axis=0))
    rows = [own_stats, others, pair_stats[1:], *stats]
    stats = jnp.concatenate(rows, axis=0).reshape(16, 2, block)
    stats = jnp.transpose(stats, (0, 2, 1)).reshape(16 * block, 2)

    two = onward(one)
    three, far = onward(two), onward(two[:block], 2)
    pieces = gathered(layer_input, swap, one, two, three, far)
    grad_own = after(out_grad, two)
    grad_swap = to_core(grad_own)
    grad_one = onward(jnp.concatenate([grad_own, grad_swap], axis=0))
    grad_two = onward(after(grad_one, three, far))
    grad_three, grad_far = onward(grad_two), onward(grad_two[:block], 2)
    grad_pieces = gathered(out_grad, grad_swap, grad_one, grad_two, grad_three, grad_far)

    split = 5 * HS
    normed, *parts = projection("xy", split, place, pieces, stats, gain[None], w_qkv)
    first, second = XFirst(parts[:4]), YFirst(parts[4:])
    token = first.step1(gain)
    token = second.step1(token)
    grad_all, *parts = context_partial("y", after(place, token), grad_pieces, w_out)
    grads = YFirst(parts)
    token = first.step2(parts[0])
    token = second.step2(token)
    token = grads.step1(token)
    token = second.step3(token)
    token = grads.step2(token)
    token = grads.step3(token)
    context, d_qkv, terms = attention(place, first, second, grads, u)

    inverse = 1.0 / gain[None]

    def partial(rows):
        d_normed = lax.dot_general(d_qkv[rows], w_qkv, (((1,), (1,)), ((), ())), preferred_element_type=F32)
        means = terms[rows] * (1.0 / features)
        return (d_normed * gain[None] - means[:, 0:1] - normed[rows].astype(F32) * inverse * means[:, 1:2]).astype(BF16)

    half = normed.shape[0] // 2
    send = partial(slice(half, None))
    keep = partial(slice(0, half))
    kept = scatter_start(keep, to_core(send))
    tn = (((0,), (0,)), ((), ()))
    normed, kept = together(normed, kept)
    own, one, two, three, far = kept
    flight = [onward(far, 2), onward(three)]
    grad_wqkv = lax.dot_general(normed, d_qkv, tn, preferred_element_type=F32).astype(BF16)
    grad_wqkv, flight = together(grad_wqkv, flight)
    own, one, two = scatter_middle(own, one, two, *flight)
    gain_part = jnp.sum(grad_wqkv.astype(F32) * w_qkv.astype(F32), axis=1) / gain
    context, gain_part, own, one, two = together(context, gain_part, own, one, two)
    flight = [onward(two, 2), onward(one)]
    grad_wout = lax.dot_general(context, grad_all, tn, preferred_element_type=F32).astype(BF16)
    told = exchange(after(gain_part, grad_wout), "col")
    told, flight = together(told, flight)
    gain_grad = jnp.sum(told, axis=0)
    total = f32_sum(*scatter_end(own, *flight))
    return (total * rstd[:, None]).astype(BF16), gain_grad, grad_wqkv, grad_wout


def solution(mesh):
    in_specs = (
        P(("dp", "col"), "row"),
        P("row"),
        P("row", "col"),
        P("col", "row"),
        P(("dp", "col"), "row"),
    )
    out_specs = (
        P(("dp", "col"), "row"),
        P(("dp", "row")),
        P(("dp", "row"), "col"),
        P(("dp", "col"), "row"),
    )
    return jax.shard_map(shards, mesh=mesh, in_specs=in_specs, out_specs=out_specs, check_vma=False)
```

```python
import functools
import math

import jax
import jax.numpy as jnp
from jax import lax
from jax.experimental import pallas as pl
from jax.experimental.pallas import tpu as pltpu
from jax.sharding import PartitionSpec as P

HS = 128
EPS = 1e-05
F32 = jnp.float32
BF16 = jnp.bfloat16
QB = 512
VMEM_LIMIT = 48 * 1024 * 1024


def to_row(v, dx, dy):
    return lax.ppermute(v, "row", [(r, ((r // 2 + dx) % 4) * 2 + ((r % 2) ^ dy)) for r in range(8)])


def to_core(v):
    return lax.ppermute(v, "col", [(c, c ^ 1) for c in range(16)])


def onward(v, hops=1):
    return lax.ppermute(v, "col", [(c, ((c // 2 + hops - 2 * hops * (c % 2)) % 8) * 2 + c % 2) for c in range(16)])


def after(v, *others):
    return lax.optimization_barrier((v, *others))[0]


def together(*groups):
    return lax.optimization_barrier(groups)


ORDER = [(0, 0), (-4, 1), (1, 1), (1, 0), (2, 1), (2, 0), (3, 1), (3, 0)]
ORDER += [(0, 1), (-4, 0), (-1, 0), (-1, 1), (-2, 0), (-2, 1), (-3, 0), (-3, 1)]


def gathered(own, swap, one, two, three, far):
    return [own] + [to_core(v) for v in (far, one, two, three)] + [swap, far, one, two, three]


def exchange(v, axis):
    n = lax.axis_size(axis)
    return lax.all_to_all(jnp.broadcast_to(v[None], (n, *v.shape)), axis, 0, 0)


def f32_sum(first, *others):
    total = first.astype(F32)
    for other in others:
        total = total + other.astype(F32)
    return total


class XFirst:
    kind = "x"

    def __init__(self, parts):
        self.terms = [parts[0]] + [to_row(parts[d], d, 0) for d in (1, 2, 3)]

    def step1(self, token):
        self.terms[0] = after(self.terms[0], token)
        sent = f32_sum(*self.terms).astype(BF16)
        self.terms.append(to_row(sent, 0, 1))
        return sent

    def step2(self, token):
        self.terms[0] = after(self.terms[0], token)
        mine = f32_sum(*self.terms).astype(BF16)
        self.pieces = [mine] + [to_row(mine, -d, 0) for d in (1, 2, 3)]
        return mine


class YFirst:
    kind = "y"

    def __init__(self, parts):
        self.keep, self.come = parts[0], to_row(parts[1], 0, 1)

    def step1(self, token):
        kept = f32_sum(after(self.keep, token), self.come)
        rows = kept.shape[0] // 4
        sent = [kept[d * rows : (d + 1) * rows].astype(BF16) for d in range(4)]
        self.terms = [kept[:rows]] + [to_row(sent[d], d, 0) for d in (1, 2, 3)]
        return sent[3]

    def step2(self, token):
        self.mine = f32_sum(after(self.terms[0], token), *self.terms[1:]).astype(BF16)
        self.others = [to_row(self.mine, -d, 0) for d in (1, 2, 3)]
        return self.mine

    def step3(self, token):
        half = jnp.concatenate([after(self.mine, token), *self.others], axis=0)
        self.pieces = [half, to_row(half, 0, 1)]
        return half


def places(block):
    r, c = lax.axis_index("row"), lax.axis_index("col")
    z, core = c // 2, c % 2
    way = 1 - 2 * core
    steps = jnp.array([d for d, _ in ORDER], jnp.int32)
    other = jnp.array([o for _, o in ORDER], jnp.int32)
    starts = (((z + way * steps) % 8) * 2 + (core + other) % 2) * block
    return jnp.concatenate([starts, jnp.stack([r // 2, r % 2])]).astype(jnp.int32)


def row_parts(kind, place, partial, outs):
    x, y = place[16], place[17]
    if kind == "x":
        for d, out in enumerate(outs):
            rows = out.shape[0]
            out[...] = partial[pl.ds(pl.multiple_of(((x + d) % 4) * rows, rows), rows), :]
    else:
        for half, out in zip((y, 1 - y), outs):
            rows = out.shape[0] // 4
            for d in range(4):
                start = pl.multiple_of((half * 4 + (x + d) % 4) * rows, rows)
                out[d * rows : (d + 1) * rows, :] = partial[pl.ds(start, rows), :]


def part_shapes(kind, tokens, width):
    count = 4 if kind == "x" else 2
    return [jax.ShapeDtypeStruct((tokens // count, width), BF16)] * count


def whole(v):
    return pl.BlockSpec(v.shape, lambda i, place: (0,) * len(v.shape))


def one_step(kernel, name, place, inputs, in_specs, outs, flops, scratch=()):
    moved = sum(math.prod(v.shape) * v.dtype.itemsize for v in [*inputs, *outs])
    return pl.pallas_call(
        kernel,
        grid_spec=pltpu.PrefetchScalarGridSpec(
            num_scalar_prefetch=1,
            grid=(1,),
            in_specs=in_specs,
            out_specs=[whole(v) for v in outs],
            scratch_shapes=list(scratch),
        ),
        out_shape=outs,
        compiler_params=pltpu.CompilerParams(vmem_limit_bytes=VMEM_LIMIT),
        cost_estimate=pl.CostEstimate(flops=flops, bytes_accessed=moved, transcendentals=0),
        name=name,
    )(place, *inputs)


def context_kernel(kind, place, *refs):
    *pieces, w_ref, all_ref = refs[:12]
    outs, partial = refs[12:-1], refs[-1]
    nt = (((1,), (1,)), ((), ()))
    at = 0
    for piece in pieces:
        all_ref[at : at + piece.shape[0], :] = piece[...]
        at += piece.shape[0]
    partial[...] = lax.dot_general(all_ref[...], w_ref[...], nt, preferred_element_type=F32).astype(BF16)
    row_parts(kind, place, partial, outs)


def context_partial(kind, place, pieces, w_out):
    tokens, here = sum(p.shape[0] for p in pieces), pieces[0].shape[1]
    width = w_out.shape[0]
    outs = [jax.ShapeDtypeStruct((tokens, here), BF16), *part_shapes(kind, tokens, width)]
    inputs = [*pieces, w_out]
    return one_step(
        functools.partial(context_kernel, kind), "context_partial", place, inputs, [whole(v) for v in inputs], outs,
        2 * tokens * here * width, [pltpu.VMEM((tokens, width), BF16)],
    )


def projection_kernel(kinds, split, place, *refs):
    *pieces, stat_ref, gain_ref, w_ref, all_ref = refs[:14]
    outs, first, second = refs[14:-2], refs[-2], refs[-1]
    block = pieces[0].shape[0]
    lanes = stat_ref.shape[1]
    rows = [stat_ref[pl.ds(place[b] // block, 1), :] for b in range(16)]
    stats = jnp.concatenate(rows + [jnp.zeros((lanes - 16, lanes), F32)], axis=0).T
    at = 0
    for piece in pieces:
        for i in range(piece.shape[0] // block):
            b = at // block
            mean, rstd = stats[:block, b : b + 1], stats[block:, b : b + 1]
            x = piece[i * block : (i + 1) * block, :].astype(F32)
            all_ref[at : at + block, :] = ((x - mean) * rstd * gain_ref[...]).astype(BF16)
            at += block
    first[...] = jnp.dot(all_ref[...], w_ref[:, :split], preferred_element_type=F32).astype(BF16)
    row_parts(kinds[0], place, first, outs[:4])
    second[...] = jnp.dot(all_ref[...], w_ref[:, split:], preferred_element_type=F32).astype(BF16)
    row_parts(kinds[1], place, second, outs[4:])


def projection(kinds, split, place, pieces, stats, gain, w_qkv):
    tokens, here = sum(p.shape[0] for p in pieces), pieces[0].shape[1]
    width = w_qkv.shape[1]
    outs = [jax.ShapeDtypeStruct((tokens, here), BF16), *part_shapes(kinds[0], tokens, split)]
    outs += part_shapes(kinds[1], tokens, width - split)
    inputs = [*pieces, stats, gain, w_qkv]
    return one_step(
        functools.partial(projection_kernel, kinds, split), "projection", place, inputs, [whole(v) for v in inputs], outs,
        2 * tokens * here * width, [pltpu.VMEM((tokens, split), BF16), pltpu.VMEM((tokens, width - split), BF16)],
    )


def unpack(kind, place, pieces, column, to_ref, at):
    x, y = place[16], place[17]
    block = to_ref.shape[0] // 16
    for b in range(16):
        if kind == "x":
            piece, i = pieces[b // 4], b % 4
            of = (x + b // 4) % 4 * 4 + i
        else:
            piece, i = pieces[b // 8], b % 8
            of = (y if b < 8 else 1 - y) * 8 + (x + i // 2) % 4 * 2 + i % 2
        to = pl.ds(pl.multiple_of(place[of], block), block)
        to_ref[to, at : at + HS] = piece[i * block : (i + 1) * block, column : column + HS]


def attention_kernel(heads, kinds, counts, place, *refs):
    head = pl.program_id(0)
    u_ref, ctx_ref, dqkv_ref, term_ref, qkv, dout, dkv, dall, ctx_s = refs[-9:]
    units = refs[: counts[0]], refs[counts[0] : sum(counts)]
    split = units[0][0].shape[1]
    tokens = qkv.shape[0]
    block = tokens // 16
    scale = 1.0 / math.sqrt(HS)
    nt = (((1,), (1,)), ((), ()))
    for h in range(heads):

        @pl.when(head == h)
        def _():
            for i in range(3):
                at = (3 * h + i) * HS
                unit, at = (0, at) if at < split else (1, at - split)
                unpack(kinds[unit], place, units[unit], at, qkv, i * HS)

    unpack(kinds[2], place, refs[sum(counts) : -9], 0, dout, 0)

    dkv[...] = jnp.zeros_like(dkv)
    k_t = qkv[:, HS : 2 * HS].T
    v_t = qkv[:, 2 * HS : 3 * HS].T
    key_at = lax.broadcasted_iota(jnp.int32, (QB, QB), 0)
    query_at = lax.broadcasted_iota(jnp.int32, (QB, QB), 1)
    for i in range(tokens // QB):
        lo, hi = i * QB, (i + 1) * QB
        query = qkv[lo:hi, :HS]
        grad = dout[lo:hi, :]
        keys = qkv[:hi, HS : 2 * HS]
        values = qkv[:hi, 2 * HS : 3 * HS]
        s = lax.dot_general(keys, query, nt, preferred_element_type=F32) * (scale * math.log2(math.e))
        last = jnp.where(key_at <= query_at, s[lo:hi], -jnp.inf)
        s = jnp.concatenate([s[:lo], last], axis=0) if i else last
        powers = jnp.exp2(s - jnp.max(s, axis=0, keepdims=True))
        probs = powers * (1.0 / jnp.sum(powers, axis=0, keepdims=True))
        probs_b = probs.astype(BF16)
        d_probs = lax.dot_general(values, grad, nt, preferred_element_type=F32)
        delta = jnp.sum(probs * d_probs, axis=0, keepdims=True)
        d_scores = (probs * (d_probs - delta) * scale).astype(BF16)
        ctx_s[lo:hi, :] = jnp.dot(v_t[:, :hi], probs_b, preferred_element_type=F32).T.astype(BF16)
        dall[lo:hi, :HS] = jnp.dot(k_t[:, :hi], d_scores, preferred_element_type=F32).T.astype(BF16)
        dkv[:hi, :HS] += jnp.dot(d_scores, query, preferred_element_type=F32)
        dkv[:hi, HS:] += jnp.dot(probs_b, grad, preferred_element_type=F32)
    dall[:, HS:] = dkv[...].astype(BF16)

    for b in range(16):
        src = pl.ds(pl.multiple_of(place[b], block), block)
        to = slice(b * block, (b + 1) * block)
        piece = dall[src, :]
        dqkv_ref[to, :] = piece
        ctx_ref[to, :] = ctx_s[src, :]
        wide = piece.astype(F32)
        first = jnp.sum(wide * u_ref[...], axis=1, keepdims=True)
        second = jnp.sum(wide * qkv[src, :].astype(F32), axis=1, keepdims=True)
        lane = lax.broadcasted_iota(jnp.int32, (block, HS), 1)
        both = jnp.where(lane == 0, first, jnp.where(lane == 1, second, 0.0))

        @pl.when(head == 0)
        def _():
            term_ref[to, :] = both

        @pl.when(head > 0)
        def _():
            term_ref[to, :] += both


def attention(place, first, second, grads, u):
    tokens = sum(p.shape[0] for p in grads.pieces)
    heads = u.shape[1] // (3 * HS)
    pieces = first.pieces + second.pieces
    shapes = [
        jax.ShapeDtypeStruct((tokens, heads * HS), BF16),
        jax.ShapeDtypeStruct((tokens, heads * 3 * HS), BF16),
        jax.ShapeDtypeStruct((tokens, HS), F32),
    ]

    def by_head(rows, cols):
        return pl.BlockSpec((rows, cols), lambda h, place: (0, h))

    return pl.pallas_call(
        functools.partial(
            attention_kernel, heads, (first.kind, second.kind, grads.kind), (len(first.pieces), len(second.pieces))
        ),
        grid_spec=pltpu.PrefetchScalarGridSpec(
            num_scalar_prefetch=1,
            grid=(heads,),
            in_specs=[whole(p) for p in pieces] + [by_head(p.shape[0], HS) for p in grads.pieces] + [by_head(1, 3 * HS)],
            out_specs=[by_head(tokens, HS), by_head(tokens, 3 * HS), pl.BlockSpec((tokens, HS), lambda h, place: (0, 0))],
            scratch_shapes=[
                pltpu.VMEM((tokens, 3 * HS), BF16),
                pltpu.VMEM((tokens, HS), BF16),
                pltpu.VMEM((tokens, 2 * HS), F32),
                pltpu.VMEM((tokens, 3 * HS), BF16),
                pltpu.VMEM((tokens, HS), BF16),
            ],
        ),
        out_shape=shapes,
        compiler_params=pltpu.CompilerParams(vmem_limit_bytes=VMEM_LIMIT),
        cost_estimate=pl.CostEstimate(
            flops=heads * tokens * tokens * HS * 12 * 5 // 8,
            bytes_accessed=heads * tokens * HS * 20,
            transcendentals=heads * tokens * tokens * 5 // 8,
        ),
        name="attention",
    )(place, *pieces, *grads.pieces, u)


def scatter_start(keep, come):
    block = keep.shape[0] // 8
    kept = f32_sum(keep, come)
    own, far, one, two, three = jnp.split(kept, [block, 2 * block, 4 * block, 6 * block], axis=0)
    return own, one, two, three.astype(BF16), far.astype(BF16)


def scatter_middle(own, one, two, far_come, three_come):
    block = own.shape[0]
    two = two + three_come.astype(F32)
    two = jnp.concatenate([two[:block] + far_come.astype(F32), two[block:]], axis=0)
    return own, one.astype(BF16), two.astype(BF16)


def scatter_end(own, two_come, one_come):
    block = own.shape[0]
    come = f32_sum(two_come, one_come)
    return own + come[block:], to_core(come[:block].astype(BF16))


def shards(layer_input, gain, w_qkv, w_out, out_grad):
    block, here = layer_input.shape
    features = here * lax.axis_size("row")
    place = places(block)

    swap = to_core(layer_input)
    pair = jnp.concatenate([layer_input, swap], axis=0)

    x = layer_input.astype(F32)
    mean_here = jnp.sum(x, axis=1) / here
    apart = x - mean_here[:, None]
    squares_here = jnp.sum(apart * apart, axis=1)
    u_here = jnp.sum(w_qkv.astype(F32) * gain[:, None], axis=0)
    told_here = after(jnp.broadcast_to(jnp.concatenate([mean_here, squares_here, u_here])[None], (8, 2*block+u_here.shape[0])), pair)
    one, told = lax.optimization_barrier((onward(pair), lax.all_to_all(told_here, "row", 0, 0)))
    means, squares = told[:, :block], told[:, block : 2 * block]
    mean = jnp.mean(means, axis=0)
    variance = (jnp.sum(squares, axis=0) + here * jnp.sum((means - mean) ** 2, axis=0)) / features
    rstd = lax.rsqrt(variance + EPS)
    u = jnp.sum(told[:, 2 * block :], axis=0)[None]
    own_stats = jnp.concatenate([mean, rstd])

    grad_swap = to_core(out_grad)
    grad_pair = jnp.concatenate([out_grad, grad_swap], axis=0)
    two, grad_one, stats = together(onward(one), onward(after(grad_pair, own_stats)), exchange(own_stats, "col"))
    three, far = together(onward(two), onward(two[:block], 2))
    pieces = gathered(layer_input, swap, one, two, three, far)
    grad_two = onward(after(grad_one, three, far))
    grad_three, grad_far = onward(grad_two), onward(grad_two[:block], 2)
    grad_pieces = gathered(out_grad, grad_swap, grad_one, grad_two, grad_three, grad_far)

    split = 5 * HS
    normed, *parts = projection("xy", split, place, pieces, stats, gain[None], w_qkv)
    first, second = XFirst(parts[:4]), YFirst(parts[4:])
    token = first.step1(gain)
    token = second.step1(token)
    grad_all, *parts = context_partial("y", after(place, token), grad_pieces, w_out)
    grads = YFirst(parts)
    token = first.step2(parts[0])
    token = second.step2(token)
    token = grads.step1(token)
    token = second.step3(token)
    token = grads.step2(token)
    token = grads.step3(token)
    context, d_qkv, terms = attention(place, first, second, grads, u)

    inverse = 1.0 / gain[None]

    def partial(rows):
        d_normed = lax.dot_general(d_qkv[rows], w_qkv, (((1,), (1,)), ((), ())), preferred_element_type=F32)
        means = terms[rows] * (1.0 / features)
        return (d_normed * gain[None] - means[:, 0:1] - normed[rows].astype(F32) * inverse * means[:, 1:2]).astype(BF16)

    half = normed.shape[0] // 2
    send = partial(slice(half, None))
    keep = partial(slice(0, half))
    kept = scatter_start(keep, to_core(send))
    tn = (((0,), (0,)), ((), ()))
    normed, kept = together(normed, kept)
    own, one, two, three, far = kept
    flight = [onward(far, 2), onward(three)]
    grad_wqkv = lax.dot_general(normed, d_qkv, tn, preferred_element_type=F32).astype(BF16)
    grad_wqkv, flight = together(grad_wqkv, flight)
    own, one, two = scatter_middle(own, one, two, *flight)
    gain_part = jnp.sum(grad_wqkv.astype(F32) * w_qkv.astype(F32), axis=1) / gain
    context, gain_part, own, one, two = together(context, gain_part, own, one, two)
    flight = [onward(two, 2), onward(one)]
    grad_wout = lax.dot_general(context, grad_all, tn, preferred_element_type=F32).astype(BF16)
    told = exchange(after(gain_part, grad_wout), "col")
    told, flight = together(told, flight)
    gain_grad = jnp.sum(told, axis=0)
    total = f32_sum(*scatter_end(own, *flight))
    return (total * rstd[:, None]).astype(BF16), gain_grad, grad_wqkv, grad_wout


def solution(mesh):
    in_specs = (
        P(("dp", "col"), "row"),
        P("row"),
        P("row", "col"),
        P("col", "row"),
        P(("dp", "col"), "row"),
    )
    out_specs = (
        P(("dp", "col"), "row"),
        P(("dp", "row")),
        P(("dp", "row"), "col"),
        P(("dp", "col"), "row"),
    )
    return jax.shard_map(shards, mesh=mesh, in_specs=in_specs, out_specs=out_specs, check_vma=False)
```
